32 devices in a mesh: bead: 8 (over y, x, core), atom: 4 (over z).
Axes of the slice: x: 2, y: 2, z: 4, core: 2. Of those that a mesh axis runs over, the one named last changes fastest.
Arguments:
- replica_point_fractions: float32 [128, 3, 6144], P('bead', None, 'atom'), may hold values from -1 to 2, as said below
- inverse_lattice_integers: int32 [3, 2048], P(None, 'bead'), may hold values from -10 to 10, as said below
- point_species_labels: int32 [6144], P('atom'), may hold values from 0 to 3
- species_electric_values: float32 [4], replicated, may hold values from -1 to 1
Outputs:
- bead_forces: float32 [128, 3, 6144], P('bead', None, 'atom')
The draws below stay inside these ranges and needn't reach their ends.
Inputs may be any that keep to these rules, and one draw needn't show every extreme that they name: replica_point_fractions holds a site's position near a common centre in all beads, with its own offset in each bead. `inverse_lattice_integers`: its columns are distinct, none is all zeros, and none is the negative of another (the first nonzero entry of each column is positive).
All inputs are finite; a program needn't handle non-finite values.
Results may differ from the reference program's by a relative error of at most 0.0003.
Values sent between devices are 32-bit elements; how exact they have to be, the bound alone decides.
A program may use at most 64 MiB of HBM per device.

```python
import math
import jax
import jax.numpy as jnp
from jax import lax

BEADS = 128
CONTR = 8
KVEC = 2048
KINDS = 4
NSITES = 6144


def draw_replica_point_fractions(key, part):
    centre_key = jax.random.fold_in(key, 11)
    offset_key = jax.random.fold_in(key, 12)
    centre = jax.random.uniform(centre_key, (1, 3, NSITES), jnp.float32, 0.0, 1.0)
    offset = 0.08 * jax.random.normal(offset_key, (BEADS, 3, NSITES), jnp.float32)
    return (centre + offset).astype(jnp.float32)


def draw_inverse_lattice_integers(key, part):
    side = 21
    total = side * side * side
    index = jnp.arange(total, dtype=jnp.int32)
    first = index // (side * side) - 10
    second = index // side % side - 10
    third = index % side - 10
    upper = (first > 0) | (first == 0) & (second > 0) | (first == 0) & (second == 0) & (third > 0)
    order = jax.random.permutation(jax.random.fold_in(key, 21), total).astype(jnp.int32)
    rank = jnp.zeros((total,), jnp.int32).at[order].set(index)
    score = jnp.where(upper, rank, rank + total)
    chosen = jnp.argsort(score, stable=True)[:KVEC]
    return jnp.stack([first[chosen], second[chosen], third[chosen]]).astype(jnp.int32)


def set_ends(drawn, stream_key, low, largest):
    place = [jax.random.randint(jax.random.fold_in(stream_key, axis), (), 0, length) for axis, length in enumerate(drawn.shape)]
    main_axis = drawn.shape.index(max(drawn.shape))
    next_to = place[:main_axis] + [(place[main_axis] + 1) % drawn.shape[main_axis]] + place[main_axis + 1:]
    return drawn.at[tuple(place)].set(low).at[tuple(next_to)].set(largest)


def setup_inputs(seed: int = 0) -> dict:
    splits = jax.random.split(jax.random.key(seed), 5)
    replica_point_fractions = draw_replica_point_fractions(jax.random.fold_in(splits[4], 71), 0)
    inverse_lattice_integers = draw_inverse_lattice_integers(jax.random.fold_in(splits[4], 71), 0)
    point_species_labels = set_ends(jax.random.randint(splits[2], (NSITES,), 0, KINDS), jax.random.fold_in(splits[2], 1), 0, KINDS - 1).astype(jnp.int32)
    species_electric_values = jnp.clip(jax.random.uniform(splits[3], (KINDS,), jnp.float32, -1.0, 1.0), -1.0, 1.0)
    return dict(replica_point_fractions=replica_point_fractions, inverse_lattice_integers=inverse_lattice_integers, point_species_labels=point_species_labels, species_electric_values=species_electric_values)


TWO_PI = 2.0 * math.pi

def cycle_modes(length, count):
    index = jnp.arange(length, dtype=jnp.float32)
    rows = [jnp.ones((length,), jnp.float32) / math.sqrt(length)]
    for mode in range(1, count // 2):
        rows.append(math.sqrt(2.0 / length) * jnp.cos(TWO_PI * mode * index / length))
        rows.append(math.sqrt(2.0 / length) * jnp.sin(TWO_PI * mode * index / length))
    if length == count:
        rows.append(jnp.cos(math.pi * index) / math.sqrt(length))
    else:
        rows.append(math.sqrt(2.0 / length) * jnp.cos(TWO_PI * (count // 2) * index / length))
    return jnp.stack(rows)

def contraction_table(beads, contr):
    small = cycle_modes(contr, contr)
    big = cycle_modes(beads, contr)
    return math.sqrt(contr / beads) * jnp.dot(small.T, big, precision=lax.Precision.HIGHEST)

def reference(replica_point_fractions, inverse_lattice_integers, point_species_labels, species_electric_values):
    table = contraction_table(BEADS, CONTR)
    contracted = jnp.einsum('jb,bxs->jxs', table, replica_point_fractions, precision=lax.Precision.HIGHEST)
    kinds = jnp.arange(species_electric_values.shape[0], dtype=jnp.int32)
    charge = lax.optimization_barrier(jnp.sum((point_species_labels[None, :] == kinds[:, None]).astype(jnp.float32) * species_electric_values[:, None], axis=0))
    fourier_mode_table = inverse_lattice_integers.astype(jnp.float32)
    square = lax.optimization_barrier(jnp.sum(fourier_mode_table * fourier_mode_table, axis=0))
    fourier_mode_factor = 4.0 * jnp.exp(-square / 100.0) / (square * NSITES)
    block = min(256, KVEC)
    nblocks = KVEC // block
    wave_blocks = jnp.transpose(fourier_mode_table.reshape(3, nblocks, block), (1, 0, 2))
    weight_blocks = fourier_mode_factor.reshape(nblocks, block)

    def per_bead(position):

        def factor_block(wave):
            angle = TWO_PI * jnp.dot(wave.T, position, precision=lax.Precision.HIGHEST)
            return (jnp.dot(jnp.cos(angle), charge, precision=lax.Precision.HIGHEST), jnp.dot(jnp.sin(angle), charge, precision=lax.Precision.HIGHEST))
        cos_fac, sin_fac = lax.map(factor_block, wave_blocks)

        def force_block(total, items):
            wave, wgt, cfac, sfac = items
            angle = TWO_PI * jnp.dot(wave.T, position, precision=lax.Precision.HIGHEST)
            left = TWO_PI * wave * (wgt * cfac)[None, :]
            right = TWO_PI * wave * (wgt * sfac)[None, :]
            term = jnp.dot(left, jnp.sin(angle), precision=lax.Precision.HIGHEST) - jnp.dot(right, jnp.cos(angle), precision=lax.Precision.HIGHEST)
            return (total + term, None)
        start = jnp.zeros((3, position.shape[1]), jnp.float32)
        total, unused = lax.scan(force_block, start, (wave_blocks, weight_blocks, cos_fac, sin_fac))
        return charge[None, :] * total
    force = lax.map(per_bead, contracted)
    return jnp.einsum('jb,jxs->bxs', table, force, precision=lax.Precision.HIGHEST)
```

```python
import functools
import math

import jax
import jax.numpy as jnp
import numpy as np
from jax import lax
from jax.experimental import pallas as pl
from jax.experimental.pallas import tpu as pltpu
from jax.sharding import PartitionSpec as P

CONTR = 8
REACH = 10
ROWS = 24
HALF = 16
GRID = HALF + REACH * ROWS
TWO_PI = 2.0 * math.pi
MESH = pl.DeviceIdType.MESH
LANES = 128


def _sine_coefficients():
    u = np.cos(np.pi * (np.arange(400) + 0.5) / 400)
    square = 0.125 + 0.125 * u
    r = np.sqrt(square)
    value = np.sin(2 * np.pi * r) / (r * (0.25 - square))
    return [float(c) for c in np.polynomial.polynomial.polyfit(square, value, 5)]


SINE = _sine_coefficients()


def sin_turns(turns):
    r = turns - jnp.round(turns)
    square = r * r
    p = SINE[5]
    for c in SINE[4::-1]:
        p = p * square + c
    return r * (0.25 - square) * p


def cos_turns(turns):
    return sin_turns(turns + 0.25)


def split(value):
    high = value.astype(jnp.bfloat16)
    low = (value - high.astype(jnp.float32)).astype(jnp.bfloat16)
    return high, low


def cycle_table(j, b, beads):
    shift = j / CONTR - b / beads
    total = jnp.ones_like(shift)
    for c in range(1, CONTR // 2):
        total = total + 2.0 * cos_turns(c * shift)
    last = cos_turns(0.5 * j) * cos_turns((CONTR // 2) * b / beads)
    total = total + math.sqrt(2.0) * last
    return total / beads


def dot_nn(a, b):
    return lax.dot_general(a, b, (((1,), (0,)), ((), ())), preferred_element_type=jnp.float32)


def dot_nt(a, b):
    return lax.dot_general(a, b, (((1,), (1,)), ((), ())), preferred_element_type=jnp.float32)


def kernel(
    nb, na, values_ref, pos_ref, wave_ref, label_ref, out_ref,
    part, land, site, waves, charge, xy_high, xy_low, z_mat, z_wave, factor, factor_land, force,
    send_wave, recv_wave, send_part, recv_part, send_fac, recv_fac, send_force, recv_force,
):
    share = nb // CONTR
    local_beads, sites = pos_ref.shape[1], pos_ref.shape[2]
    beads = local_beads * nb
    own_sites = sites // share
    tiles = own_sites // LANES
    rows = part.shape[1]
    kvec = wave_ref.shape[1]
    group = na * share
    me = lax.axis_index("bead")
    atom = lax.axis_index("atom")
    bead, chunk = me // share, lax.rem(me, share)

    def bead_peer(d):
        return (lax.rem(me + d, nb), atom)

    def group_peer(d):
        other = bead * share + lax.rem(chunk + d % share, share)
        return (other, lax.rem(atom + d // share, na))

    barrier = pltpu.get_barrier_semaphore()
    peers = [bead_peer(d) for d in range(1, nb)]
    peers += [group_peer(d) for d in range(1, group) if d >= share]
    for peer in peers:
        pl.semaphore_signal(barrier, inc=1, device_id=peer, device_id_type=MESH)

    waves[me] = jnp.zeros((8, kvec), jnp.float32)
    waves[me, 0:3, :] = wave_ref[...].astype(jnp.float32)

    lane = lax.broadcasted_iota(jnp.int32, (8, LANES), 1)
    sub = lax.broadcasted_iota(jnp.int32, (8, LANES), 0)
    first = me * local_beads
    table = cycle_table(sub.astype(jnp.float32), (first + lane).astype(jnp.float32), beads)
    columns = [jnp.broadcast_to(table[:, b : b + 1], (8, LANES)) for b in range(local_beads)]
    for x in range(3):
        for t in range(sites // LANES):
            total = None
            for b in range(local_beads):
                term = columns[b] * pos_ref[x, b : b + 1, t * LANES : (t + 1) * LANES]
                total = term if total is None else total + term
            c, row = t // tiles, x * tiles + t % tiles
            for j in range(CONTR):
                part[j * share + c, row : row + 1, :] = total[j : j + 1, :]

    pl.semaphore_wait(barrier, len(peers))

    part_copies, wave_copies = [], []
    for d in range(1, nb):
        peer = bead_peer(d)
        copy = pltpu.make_async_remote_copy(
            src_ref=part.at[peer[0]], dst_ref=land.at[d], send_sem=send_part.at[d],
            recv_sem=recv_part.at[d], device_id=peer, device_id_type=MESH,
        )
        copy.start()
        part_copies.append(copy)
    for d in range(1, nb):
        copy = pltpu.make_async_remote_copy(
            src_ref=waves.at[me], dst_ref=waves.at[me], send_sem=send_wave.at[d],
            recv_sem=recv_wave.at[d], device_id=bead_peer(d), device_id_type=MESH,
        )
        copy.start()
        wave_copies.append(copy)

    label = label_ref[...]
    q = jnp.zeros(label.shape, jnp.float32)
    for kind in range(values_ref.shape[0]):
        q = q + jnp.where(label == kind, values_ref[kind], 0.0)
    for c in range(share):
        charge[c, 0:tiles, :] = q[c * tiles : (c + 1) * tiles, :]

    for copy in part_copies:
        copy.wait()
    total = part[me]
    for d in range(1, nb):
        total = total + land[d]
    site[...] = total

    row_id = lax.broadcasted_iota(jnp.int32, (ROWS, LANES), 0)
    second = jnp.where(row_id < ROWS - REACH, row_id, row_id - ROWS).astype(jnp.float32)
    third = (row_id - REACH).astype(jnp.float32)

    def reduced(row):
        x = site[pl.ds(row, 1), :]
        return x - jnp.round(x)

    def build(t, carry):
        where = pl.ds(pl.multiple_of(t * LANES, LANES), LANES)
        x = jnp.broadcast_to(reduced(t), (ROWS, LANES))
        y = second * reduced(tiles + t)
        z = third * reduced(2 * tiles + t)
        step_r, step_i = cos_turns(x), sin_turns(x)
        real, imag = cos_turns(y), sin_turns(y)
        reals, imags = [real[:HALF]], [imag[:HALF]]
        for a in range(REACH):
            real, imag = real * step_r - imag * step_i, real * step_i + imag * step_r
            reals.append(real)
            imags.append(imag)
        for base, parts in ((0, reals), (GRID, imags)):
            blocks = [parts[0]]
            for a in range(1, REACH + 1, 2):
                blocks.append(jnp.concatenate(parts[a : a + 2], axis=0))
            at = base
            for block in blocks:
                high, low = split(block)
                xy_high[at : at + block.shape[0], where] = high
                xy_low[at : at + block.shape[0], where] = low
                at += block.shape[0]
        cos_z, sin_z = cos_turns(z), sin_turns(z)
        z_wave[0, :, where] = cos_z
        z_wave[1, :, where] = sin_z
        q_row = charge[chunk, pl.ds(t, 1), :]
        qc, qs = q_row * cos_z, q_row * sin_z
        for n, block in enumerate(((qc, qs), (-qs, qc))):
            high, low = split(jnp.concatenate(block, axis=0))
            z_mat[n, 0 : 2 * ROWS, where] = high
            z_mat[n, 2 * ROWS : 4 * ROWS, where] = low
        return carry

    lax.fori_loop(0, tiles, build, 0)

    product = dot_nt(z_mat[0], xy_high[0:GRID, :]) + dot_nt(z_mat[1], xy_high[GRID : 2 * GRID, :])
    own = product[: 2 * ROWS] + product[2 * ROWS :]
    own = own + dot_nt(z_mat[0, 0 : 2 * ROWS, :], xy_low[0:GRID, :])
    own = own + dot_nt(z_mat[1, 0 : 2 * ROWS, :], xy_low[GRID : 2 * GRID, :])
    factor[...] = own

    factor_copies = []
    for d in range(1, group):
        copy = pltpu.make_async_remote_copy(
            src_ref=factor, dst_ref=factor_land.at[d], send_sem=send_fac.at[d],
            recv_sem=recv_fac.at[d], device_id=group_peer(d), device_id_type=MESH,
        )
        copy.start()
        factor_copies.append(copy)

    for copy in wave_copies:
        copy.wait()
    count = jnp.zeros((ROWS, GRID), jnp.float32)
    pair_id = lax.broadcasted_iota(jnp.int32, (GRID, kvec), 0).astype(jnp.float32)
    third_id = lax.broadcasted_iota(jnp.int32, (ROWS, kvec), 0).astype(jnp.float32)
    for n in range(nb):
        m = waves[n]
        m0, m1, m2 = m[0:1], m[1:2], m[2:3]
        wrapped = jnp.where(m1 < 0.0, m1 + ROWS, m1)
        pair = jnp.where(m0 > 0.0, HALF + (m0 - 1.0) * ROWS + wrapped, m1)
        hot_pair = jnp.where(pair_id == pair, 1.0, 0.0).astype(jnp.bfloat16)
        hot_third = jnp.where(third_id == m2 + REACH, 1.0, 0.0).astype(jnp.bfloat16)
        count = count + dot_nt(hot_third, hot_pair)
    col = lax.broadcasted_iota(jnp.int32, (ROWS, GRID), 1)
    line = lax.broadcasted_iota(jnp.int32, (ROWS, GRID), 0)
    f0 = jnp.zeros((ROWS, GRID), jnp.int32)
    for a in range(REACH):
        f0 = f0 + jnp.where(col >= HALF + a * ROWS, 1, 0)
    f1 = jnp.where(f0 > 0, col - HALF - (f0 - 1) * ROWS, col)
    f1 = jnp.where(f1 < ROWS - REACH, f1, f1 - ROWS)
    f2 = line - REACH
    f0, f1, f2 = f0.astype(jnp.float32), f1.astype(jnp.float32), f2.astype(jnp.float32)
    msq = f0 * f0 + f1 * f1 + f2 * f2
    weight = 4.0 * jnp.exp(-msq / 100.0) / (jnp.maximum(msq, 1.0) * float(sites * na))
    weight = weight * count

    for copy in factor_copies:
        copy.wait()
    total = factor[...]
    for d in range(1, group):
        total = total + factor_land[d]
    gr, gi = weight * total[:ROWS], weight * total[ROWS:]
    u, v = jnp.concatenate([-gi, gr], axis=1), jnp.concatenate([gr, gi], axis=1)
    w0, w1 = jnp.concatenate([f0, f0], axis=1), jnp.concatenate([f1, f1], axis=1)
    left = jnp.concatenate([u, v, w0 * u, w0 * v, w1 * u, w1 * v], axis=0)
    left_high, left_low = split(left)
    left_both = jnp.concatenate([left_high, left_low], axis=0)
    height = 6 * ROWS

    width = 2 * LANES if tiles % 2 == 0 else LANES
    per = width // LANES
    m2_rows = (lax.broadcasted_iota(jnp.int32, (ROWS, width), 0) - REACH).astype(jnp.float32)
    for n in range(own_sites // width):
        where = slice(n * width, (n + 1) * width)
        both = dot_nn(left_both, xy_high[:, where])
        term = both[:height] + both[height:] + dot_nn(left_high, xy_low[:, where])
        cz, sz = z_wave[0, :, where], z_wave[1, :, where]
        pieces = [
            term[2 * i * ROWS : (2 * i + 1) * ROWS] * cz
            + term[(2 * i + 1) * ROWS : (2 * i + 2) * ROWS] * sz
            for i in range(3)
        ]
        along = (pieces[1], pieces[2], pieces[0] * m2_rows)
        for x in range(3):
            summed = TWO_PI * jnp.sum(along[x], axis=0, keepdims=True)
            for p in range(per):
                t = n * per + p
                q_row = charge[chunk, t : t + 1, :]
                force[me, x * tiles + t : x * tiles + t + 1, :] = (
                    q_row * summed[:, p * LANES : (p + 1) * LANES]
                )

    force_copies = []
    for d in range(1, nb):
        copy = pltpu.make_async_remote_copy(
            src_ref=force.at[me], dst_ref=force.at[me], send_sem=send_force.at[d],
            recv_sem=recv_force.at[d], device_id=bead_peer(d), device_id_type=MESH,
        )
        copy.start()
        force_copies.append(copy)
    sub_b = lax.broadcasted_iota(jnp.int32, (local_beads, LANES), 0)
    lane_j = lax.broadcasted_iota(jnp.int32, (local_beads, LANES), 1)
    turned = cycle_table(lane_j.astype(jnp.float32), (first + sub_b).astype(jnp.float32), beads)
    spread = [jnp.broadcast_to(turned[:, j : j + 1], (local_beads, LANES)) for j in range(CONTR)]
    for copy in force_copies:
        copy.wait()
    for x in range(3):
        for t in range(sites // LANES):
            c, row = t // tiles, x * tiles + t % tiles
            total = None
            for j in range(CONTR):
                term = spread[j] * force[j * share + c, row : row + 1, :]
                total = term if total is None else total + term
            out_ref[x, :, t * LANES : (t + 1) * LANES] = total


def local(nb, na, positions, waves, labels, values):
    local_beads, _, sites = positions.shape
    kvec = waves.shape[1]
    share = nb // CONTR
    own_sites = sites // share
    tiles = own_sites // LANES
    rows = -(-3 * tiles // 8) * 8
    group = na * share
    dma = pltpu.SemaphoreType.DMA
    vmem = pl.BlockSpec(memory_space=pltpu.VMEM)
    out = pl.pallas_call(
        functools.partial(kernel, nb, na),
        out_shape=jax.ShapeDtypeStruct((3, local_beads, sites), jnp.float32),
        in_specs=[pl.BlockSpec(memory_space=pltpu.SMEM), vmem, vmem, vmem],
        out_specs=vmem,
        scratch_shapes=[
            pltpu.VMEM((nb, rows, LANES), jnp.float32),
            pltpu.VMEM((nb, rows, LANES), jnp.float32),
            pltpu.VMEM((rows, LANES), jnp.float32),
            pltpu.VMEM((nb, 8, kvec), jnp.float32),
            pltpu.VMEM((share, -(-tiles // 8) * 8, LANES), jnp.float32),
            pltpu.VMEM((2 * GRID, own_sites), jnp.bfloat16),
            pltpu.VMEM((2 * GRID, own_sites), jnp.bfloat16),
            pltpu.VMEM((2, 4 * ROWS, own_sites), jnp.bfloat16),
            pltpu.VMEM((2, ROWS, own_sites), jnp.float32),
            pltpu.VMEM((2 * ROWS, GRID), jnp.float32),
            pltpu.VMEM((group, 2 * ROWS, GRID), jnp.float32),
            pltpu.VMEM((nb, rows, LANES), jnp.float32),
            dma((nb,)), dma((nb,)), dma((nb,)), dma((nb,)),
            dma((group,)), dma((group,)), dma((nb,)), dma((nb,)),
        ],
        compiler_params=pltpu.CompilerParams(
            collective_id=0, has_side_effects=True, vmem_limit_bytes=40 * 1024 * 1024
        ),
    )(values, jnp.transpose(positions, (1, 0, 2)), waves, labels.reshape(-1, LANES))
    return jnp.transpose(out, (1, 0, 2))


def solution(mesh):
    in_specs = (P("bead", None, "atom"), P(None, "bead"), P("atom"), P())
    out_specs = P("bead", None, "atom")
    body = functools.partial(local, mesh.shape["bead"], mesh.shape["atom"])
    return jax.shard_map(body, mesh=mesh, in_specs=in_specs, out_specs=out_specs, check_vma=False)
```

```python
import functools
import math

import jax
import jax.numpy as jnp
import numpy as np
from jax import lax
from jax.experimental import pallas as pl
from jax.experimental.pallas import tpu as pltpu
from jax.sharding import PartitionSpec as P

CONTR = 8
REACH = 10
ROWS = 24
HALF = 16
GRID = HALF + REACH * ROWS
TWO_PI = 2.0 * math.pi
MESH = pl.DeviceIdType.MESH
LANES = 128


def _sine_coefficients():
    u = np.cos(np.pi * (np.arange(400) + 0.5) / 400)
    square = 0.125 + 0.125 * u
    r = np.sqrt(square)
    value = np.sin(2 * np.pi * r) / (r * (0.25 - square))
    return [float(c) for c in np.polynomial.polynomial.polyfit(square, value, 5)]


SINE = _sine_coefficients()


def sin_turns(turns):
    r = turns - jnp.round(turns)
    square = r * r
    p = SINE[5]
    for c in SINE[4::-1]:
        p = p * square + c
    return r * (0.25 - square) * p


def cos_turns(turns):
    return sin_turns(turns + 0.25)


def split(value):
    high = value.astype(jnp.bfloat16)
    low = (value - high.astype(jnp.float32)).astype(jnp.bfloat16)
    return high, low


def cycle_table(j, b, beads):
    shift = j / CONTR - b / beads
    total = jnp.ones_like(shift)
    for c in range(1, CONTR // 2):
        total = total + 2.0 * cos_turns(c * shift)
    last = cos_turns(0.5 * j) * cos_turns((CONTR // 2) * b / beads)
    total = total + math.sqrt(2.0) * last
    return total / beads


def dot_nn(a, b):
    return lax.dot_general(a, b, (((1,), (0,)), ((), ())), preferred_element_type=jnp.float32)


def dot_nt(a, b):
    return lax.dot_general(a, b, (((1,), (1,)), ((), ())), preferred_element_type=jnp.float32)


def kernel(
    nb, na, values_hbm, pos_hbm, wave_hbm, label_hbm, out_hbm,
    out_ref, values, pos, wave_in, label_in,
    part, land, site, waves, charge, xy_high, xy_low, z_mat, z_wave, factor, factor_land, whole, turned, force,
    in_sem, pos_sem, out_sem, send_wave, recv_wave, send_part, recv_part, send_fac, recv_fac, send_all, recv_all,
    send_force, recv_force,
):
    share = nb // CONTR
    local_beads, sites = pos.shape[1], pos.shape[2]
    beads = local_beads * nb
    own_sites = sites // share
    tiles = own_sites // LANES
    chunks = site.shape[0]
    span = tiles // chunks
    kvec = wave_in.shape[1]
    group = na * share
    me = lax.axis_index("bead")
    atom = lax.axis_index("atom")
    bead, chunk = me // share, lax.rem(me, share)
    place = atom * share + chunk

    def bead_peer(d):
        return (lax.rem(me + d, nb), atom)

    def group_peer(d):
        other = bead * share + lax.rem(chunk + d % share, share)
        return (other, lax.rem(atom + d // share, na))

    barrier = pltpu.get_barrier_semaphore()
    peers = [bead_peer(d) for d in range(1, nb)]
    peers += [group_peer(d) for d in range(1, group) if d >= share]
    for peer in peers:
        pl.semaphore_signal(barrier, inc=1, device_id=peer, device_id_type=MESH)

    wave_copy = pltpu.make_async_copy(wave_hbm, wave_in, in_sem.at[0])
    wave_copy.start()
    pos_copies = []
    for n in range(chunks):
        for c in range(share):
            where = pl.ds((c * tiles + n * span) * LANES, span * LANES)
            copy = pltpu.make_async_copy(
                pos_hbm.at[:, :, where], pos.at[:, :, where], pos_sem.at[n * share + c]
            )
            copy.start()
            pos_copies.append(copy)
    label_copy = pltpu.make_async_copy(label_hbm, label_in, in_sem.at[1])
    label_copy.start()
    value_copy = pltpu.make_async_copy(values_hbm, values, in_sem.at[2])
    value_copy.start()

    lane = lax.broadcasted_iota(jnp.int32, (8, LANES), 1)
    sub = lax.broadcasted_iota(jnp.int32, (8, LANES), 0)
    first = me * local_beads
    table = cycle_table(sub.astype(jnp.float32), (first + lane).astype(jnp.float32), beads)
    columns = [jnp.broadcast_to(table[:, b : b + 1], (8, LANES)) for b in range(local_beads)]

    wave_copy.wait()
    waves[me] = jnp.zeros((8, kvec), jnp.float32)
    waves[me, 0:3, :] = wave_in[...].astype(jnp.float32)

    part_copies, wave_copies = [], []
    for n in range(chunks):
        for c in range(share):
            pos_copies[n * share + c].wait()
            for x in range(3):
                for t in range(span):
                    at = (c * tiles + n * span + t) * LANES
                    total = None
                    for b in range(local_beads):
                        term = columns[b] * pos[x, b : b + 1, at : at + LANES]
                        total = term if total is None else total + term
                    row = x * span + t
                    for j in range(CONTR):
                        part[j * share + c, n, row : row + 1, :] = total[j : j + 1, :]
        if n == 0:
            pl.semaphore_wait(barrier, len(peers))
        for d in range(1, nb):
            peer = bead_peer(d)
            copy = pltpu.make_async_remote_copy(
                src_ref=part.at[peer[0], n], dst_ref=land.at[d, n], send_sem=send_part.at[n, d],
                recv_sem=recv_part.at[n, d], device_id=peer, device_id_type=MESH,
            )
            copy.start()
            part_copies.append(copy)
    for d in range(1, nb):
        copy = pltpu.make_async_remote_copy(
            src_ref=waves.at[me], dst_ref=waves.at[me], send_sem=send_wave.at[d],
            recv_sem=recv_wave.at[d], device_id=bead_peer(d), device_id_type=MESH,
        )
        copy.start()
        wave_copies.append(copy)

    label_copy.wait()
    value_copy.wait()
    label = label_in[...]
    q = jnp.zeros(label.shape, jnp.float32)
    for kind in range(values.shape[0]):
        q = q + jnp.where(label == kind, values[kind], 0.0)
    for c in range(share):
        charge[c, 0:tiles, :] = q[c * tiles : (c + 1) * tiles, :]
    sub_b = lax.broadcasted_iota(jnp.int32, (local_beads, LANES), 0)
    lane_j = lax.broadcasted_iota(jnp.int32, (local_beads, LANES), 1)
    turned[...] = cycle_table(
        lane_j.astype(jnp.float32), (first + sub_b).astype(jnp.float32), beads
    )

    row_id = lax.broadcasted_iota(jnp.int32, (ROWS, LANES), 0)
    second = jnp.where(row_id < ROWS - REACH, row_id, row_id - ROWS).astype(jnp.float32)
    third = (row_id - REACH).astype(jnp.float32)

    for n in range(chunks):
        for copy in part_copies[n * (nb - 1) : (n + 1) * (nb - 1)]:
            copy.wait()
        total = part[me, n]
        for d in range(1, nb):
            total = total + land[d, n]
        site[n] = total - jnp.round(total)

        def build(t, carry, n=n):
            where = pl.ds(pl.multiple_of((n * span + t) * LANES, LANES), LANES)
            x = site[n, pl.ds(t, 1), :]
            step_r = jnp.broadcast_to(cos_turns(x), (ROWS, LANES))
            step_i = jnp.broadcast_to(sin_turns(x), (ROWS, LANES))
            y = second * site[n, pl.ds(span + t, 1), :]
            z = third * site[n, pl.ds(2 * span + t, 1), :]
            real, imag = cos_turns(y), sin_turns(y)
            reals, imags = [real[:HALF]], [imag[:HALF]]
            for a in range(REACH):
                real, imag = real * step_r - imag * step_i, real * step_i + imag * step_r
                reals.append(real)
                imags.append(imag)
            for base, parts in ((0, reals), (GRID, imags)):
                blocks = [parts[0]]
                for a in range(1, REACH + 1, 2):
                    blocks.append(jnp.concatenate(parts[a : a + 2], axis=0))
                at = base
                for block in blocks:
                    high, low = split(block)
                    xy_high[at : at + block.shape[0], where] = high
                    xy_low[at : at + block.shape[0], where] = low
                    at += block.shape[0]
            cos_z, sin_z = cos_turns(z), sin_turns(z)
            z_wave[0, :, where] = cos_z
            z_wave[1, :, where] = sin_z
            q_row = charge[chunk, pl.ds(n * span + t, 1), :]
            qc, qs = q_row * cos_z, q_row * sin_z
            for i, block in enumerate(((qc, qs), (-qs, qc))):
                high, low = split(jnp.concatenate(block, axis=0))
                z_mat[i, 0 : 2 * ROWS, where] = high
                z_mat[i, 2 * ROWS : 4 * ROWS, where] = low
            return carry

        lax.fori_loop(0, span, build, 0)

    pieces = factor_land.shape[1]
    count_tiles = 2 * ROWS * GRID // (8 * LANES)
    product = dot_nt(z_mat[0], xy_high[0:GRID, :]) + dot_nt(z_mat[1], xy_high[GRID : 2 * GRID, :])
    own = product[: 2 * ROWS] + product[2 * ROWS :]
    own = own + dot_nt(z_mat[0, 0 : 2 * ROWS, :], xy_low[0:GRID, :])
    own = own + dot_nt(z_mat[1, 0 : 2 * ROWS, :], xy_low[GRID : 2 * GRID, :])
    for l in range(GRID // LANES):
        for i in range(2 * ROWS // 8):
            factor[l * (2 * ROWS // 8) + i] = own[8 * i : 8 * i + 8, l * LANES : (l + 1) * LANES]
    for i in range(count_tiles, group * pieces):
        factor[i] = jnp.zeros((8, LANES), jnp.float32)
    factor_copies = []
    for d in range(1, group):
        peer = group_peer(d)
        target = peer[1] * share + lax.rem(peer[0], share)
        copy = pltpu.make_async_remote_copy(
            src_ref=factor.at[pl.ds(target * pieces, pieces)], dst_ref=factor_land.at[d],
            send_sem=send_fac.at[d], recv_sem=recv_fac.at[d], device_id=peer, device_id_type=MESH,
        )
        copy.start()
        factor_copies.append(copy)

    for copy in wave_copies:
        copy.wait()
    count = jnp.zeros((ROWS, GRID), jnp.float32)
    pair_id = lax.broadcasted_iota(jnp.int32, (GRID, kvec), 0).astype(jnp.float32)
    third_id = lax.broadcasted_iota(jnp.int32, (ROWS, kvec), 0).astype(jnp.float32)
    for n in range(nb):
        m = waves[n]
        m0, m1, m2 = m[0:1], m[1:2], m[2:3]
        wrapped = jnp.where(m1 < 0.0, m1 + ROWS, m1)
        pair = jnp.where(m0 > 0.0, HALF + (m0 - 1.0) * ROWS + wrapped, m1)
        hot_pair = jnp.where(pair_id == pair, 1.0, 0.0).astype(jnp.bfloat16)
        hot_third = jnp.where(third_id == m2 + REACH, 1.0, 0.0).astype(jnp.bfloat16)
        count = count + dot_nt(hot_third, hot_pair)

    mine = pl.ds(place * pieces, pieces)
    all_copies = []
    for copy in factor_copies:
        copy.wait()
    total = factor[mine]
    for d in range(1, group):
        total = total + factor_land[d]
    whole[mine] = total
    for d in range(1, group):
        copy = pltpu.make_async_remote_copy(
            src_ref=whole.at[mine], dst_ref=whole.at[mine], send_sem=send_all.at[d],
            recv_sem=recv_all.at[d], device_id=group_peer(d), device_id_type=MESH,
        )
        copy.start()
        all_copies.append(copy)

    col = lax.broadcasted_iota(jnp.int32, (ROWS, GRID), 1)
    line = lax.broadcasted_iota(jnp.int32, (ROWS, GRID), 0)
    f0 = jnp.zeros((ROWS, GRID), jnp.int32)
    for a in range(REACH):
        f0 = f0 + jnp.where(col >= HALF + a * ROWS, 1, 0)
    f1 = jnp.where(f0 > 0, col - HALF - (f0 - 1) * ROWS, col)
    f1 = jnp.where(f1 < ROWS - REACH, f1, f1 - ROWS)
    f2 = line - REACH
    f0, f1, f2 = f0.astype(jnp.float32), f1.astype(jnp.float32), f2.astype(jnp.float32)
    msq = f0 * f0 + f1 * f1 + f2 * f2
    weight = 4.0 * jnp.exp(-msq / 100.0) / (jnp.maximum(msq, 1.0) * float(sites * na))
    weight = weight * count
    w0, w1 = jnp.concatenate([f0, f0], axis=1), jnp.concatenate([f1, f1], axis=1)

    for copy in all_copies:
        copy.wait()
    per_lane = 2 * ROWS // 8
    half = per_lane // 2

    def gather(base):
        return jnp.concatenate(
            [
                jnp.concatenate([whole[l * per_lane + base + i] for i in range(half)], axis=0)
                for l in range(GRID // LANES)
            ],
            axis=1,
        )

    gr, gi = weight * gather(0), weight * gather(half)
    u, v = jnp.concatenate([-gi, gr], axis=1), jnp.concatenate([gr, gi], axis=1)
    left = jnp.concatenate([u, v, w0 * u, w0 * v, w1 * u, w1 * v], axis=0)
    left_high, left_low = split(left)
    left_both = jnp.concatenate([left_high, left_low], axis=0)
    height = 6 * ROWS

    width = 2 * LANES if span % 2 == 0 else LANES
    per = width // LANES
    m2_rows = (lax.broadcasted_iota(jnp.int32, (ROWS, width), 0) - REACH).astype(jnp.float32)
    force_copies = []
    for n in range(chunks):
        for k in range(span // per):
            start = (n * span + k * per) * LANES
            where = slice(start, start + width)
            both = dot_nn(left_both, xy_high[:, where])
            term = both[:height] + both[height:] + dot_nn(left_high, xy_low[:, where])
            cz, sz = z_wave[0, :, where], z_wave[1, :, where]
            blocks = [
                term[2 * i * ROWS : (2 * i + 1) * ROWS] * cz
                + term[(2 * i + 1) * ROWS : (2 * i + 2) * ROWS] * sz
                for i in range(3)
            ]
            along = (blocks[1], blocks[2], blocks[0] * m2_rows)
            for x in range(3):
                summed = TWO_PI * jnp.sum(along[x], axis=0, keepdims=True)
                for p in range(per):
                    t = k * per + p
                    q_row = charge[chunk, n * span + t : n * span + t + 1, :]
                    force[me, n, x * span + t : x * span + t + 1, :] = (
                        q_row * summed[:, p * LANES : (p + 1) * LANES]
                    )
        for d in range(1, nb):
            copy = pltpu.make_async_remote_copy(
                src_ref=force.at[me, n], dst_ref=force.at[me, n], send_sem=send_force.at[n, d],
                recv_sem=recv_force.at[n, d], device_id=bead_peer(d), device_id_type=MESH,
            )
            copy.start()
            force_copies.append(copy)

    table = turned[...]
    spread = [jnp.broadcast_to(table[:, j : j + 1], (local_beads, LANES)) for j in range(CONTR)]
    out_copies = []
    for n in range(chunks):
        for copy in force_copies[n * (nb - 1) : (n + 1) * (nb - 1)]:
            copy.wait()
        for c in range(share):
            for x in range(3):
                for t in range(span):
                    total = None
                    for j in range(CONTR):
                        row = x * span + t
                        term = spread[j] * force[j * share + c, n, row : row + 1, :]
                        total = term if total is None else total + term
                    at = (c * tiles + n * span + t) * LANES
                    out_ref[x, :, at : at + LANES] = total
            where = pl.ds((c * tiles + n * span) * LANES, span * LANES)
            copy = pltpu.make_async_copy(
                out_ref.at[:, :, where], out_hbm.at[:, :, where], out_sem.at[n * share + c]
            )
            copy.start()
            out_copies.append(copy)
    for copy in out_copies:
        copy.wait()


def local(nb, na, positions, waves, labels, values):
    local_beads, _, sites = positions.shape
    kvec = waves.shape[1]
    share = nb // CONTR
    own_sites = sites // share
    tiles = own_sites // LANES
    span = max(n for n in (1, 2, 3, 4) if tiles % n == 0)
    chunks = tiles // span
    rows = -(-3 * span // 8) * 8
    group = na * share
    pieces = -(-(2 * ROWS * GRID // (8 * LANES)) // group)
    dma = pltpu.SemaphoreType.DMA
    f32, bf16 = jnp.float32, jnp.bfloat16
    hbm = pl.BlockSpec(memory_space=pltpu.HBM)
    out = pl.pallas_call(
        functools.partial(kernel, nb, na),
        out_shape=jax.ShapeDtypeStruct((3, local_beads, sites), f32),
        in_specs=[hbm] * 4,
        out_specs=hbm,
        scratch_shapes=[
            pltpu.VMEM((3, local_beads, sites), f32),
            pltpu.SMEM(values.shape, f32),
            pltpu.VMEM((3, local_beads, sites), f32),
            pltpu.VMEM((3, kvec), jnp.int32),
            pltpu.VMEM((sites // LANES, LANES), jnp.int32),
            pltpu.VMEM((nb, chunks, rows, LANES), f32),
            pltpu.VMEM((nb, chunks, rows, LANES), f32),
            pltpu.VMEM((chunks, rows, LANES), f32),
            pltpu.VMEM((nb, 8, kvec), f32),
            pltpu.VMEM((share, -(-tiles // 8) * 8, LANES), f32),
            pltpu.VMEM((2 * GRID, own_sites), bf16),
            pltpu.VMEM((2 * GRID, own_sites), bf16),
            pltpu.VMEM((2, 4 * ROWS, own_sites), bf16),
            pltpu.VMEM((2, ROWS, own_sites), f32),
            pltpu.VMEM((group * pieces, 8, LANES), f32),
            pltpu.VMEM((group, pieces, 8, LANES), f32),
            pltpu.VMEM((group * pieces, 8, LANES), f32),
            pltpu.VMEM((local_beads, LANES), f32),
            pltpu.VMEM((nb, chunks, rows, LANES), f32),
            dma((3,)), dma((chunks * share,)), dma((chunks * share,)), dma((nb,)), dma((nb,)), dma((chunks, nb)), dma((chunks, nb)),
            dma((group,)), dma((group,)), dma((group,)), dma((group,)), dma((chunks, nb)), dma((chunks, nb)),
        ],
        compiler_params=pltpu.CompilerParams(
            collective_id=0, has_side_effects=True, vmem_limit_bytes=60 * 1024 * 1024
        ),
    )(values, jnp.transpose(positions, (1, 0, 2)), waves, labels.reshape(-1, LANES))
    return jnp.transpose(out, (1, 0, 2))


def solution(mesh):
    in_specs = (P("bead", None, "atom"), P(None, "bead"), P("atom"), P())
    out_specs = P("bead", None, "atom")
    body = functools.partial(local, mesh.shape["bead"], mesh.shape["atom"])
    return jax.shard_map(body, mesh=mesh, in_specs=in_specs, out_specs=out_specs, check_vma=False)
```

```python
import functools
import math

import jax
import jax.numpy as jnp
import numpy as np
from jax import lax
from jax.experimental import pallas as pl
from jax.experimental.pallas import tpu as pltpu
from jax.sharding import PartitionSpec as P

CONTR = 8
REACH = 10
ROWS = 24
HALF = 16
GRID = HALF + REACH * ROWS
TWO_PI = 2.0 * math.pi
MESH = pl.DeviceIdType.MESH
LANES = 128


def _sine_coefficients():
    u = np.cos(np.pi * (np.arange(400) + 0.5) / 400)
    square = 0.125 + 0.125 * u
    r = np.sqrt(square)
    value = np.sin(2 * np.pi * r) / (r * (0.25 - square))
    return [float(c) for c in np.polynomial.polynomial.polyfit(square, value, 5)]


SINE = _sine_coefficients()


def sin_turns(turns):
    r = turns - jnp.round(turns)
    square = r * r
    p = SINE[5]
    for c in SINE[4::-1]:
        p = p * square + c
    return r * (0.25 - square) * p


def cos_turns(turns):
    return sin_turns(turns + 0.25)


def split(value):
    high = value.astype(jnp.bfloat16)
    low = (value - high.astype(jnp.float32)).astype(jnp.bfloat16)
    return high, low


def cycle_table(j, b, beads):
    shift = j / CONTR - b / beads
    total = jnp.ones_like(shift)
    for c in range(1, CONTR // 2):
        total = total + 2.0 * cos_turns(c * shift)
    last = cos_turns(0.5 * j) * cos_turns((CONTR // 2) * b / beads)
    total = total + math.sqrt(2.0) * last
    return total / beads


def dot_nn(a, b):
    return lax.dot_general(a, b, (((1,), (0,)), ((), ())), preferred_element_type=jnp.float32)


def dot_nt(a, b):
    return lax.dot_general(a, b, (((1,), (1,)), ((), ())), preferred_element_type=jnp.float32)


def kernel(
    nb, na, values_hbm, pos_hbm, wave_hbm, label_hbm, gathered,
    values, pos, wave_in, label_in,
    part, land, site, waves, charge, xy_high, xy_low, z_mat, z_wave, factor, factor_land, whole, force,
    in_sem, pos_sem, send_wave, recv_wave, send_part, recv_part, send_fac, recv_fac,
    send_force, recv_force,
):
    share = nb // CONTR
    local_beads, sites = pos.shape[1], pos.shape[2]
    beads = local_beads * nb
    own_sites = sites // share
    tiles = own_sites // LANES
    chunks = site.shape[0]
    span = tiles // chunks
    kvec = wave_in.shape[1]
    group = na * share
    me = lax.axis_index("bead")
    atom = lax.axis_index("atom")
    bead, chunk = me // share, lax.rem(me, share)
    place = atom * share + chunk

    def bead_peer(d):
        return (lax.rem(me + d, nb), atom)

    def group_peer(d):
        other = bead * share + lax.rem(chunk + d % share, share)
        return (other, lax.rem(atom + d // share, na))

    barrier = pltpu.get_barrier_semaphore()
    peers = [bead_peer(d) for d in range(1, nb)]
    peers += [group_peer(d) for d in range(1, group) if d >= share]
    for peer in peers:
        pl.semaphore_signal(barrier, inc=1, device_id=peer, device_id_type=MESH)

    wave_copy = pltpu.make_async_copy(wave_hbm, wave_in, in_sem.at[0])
    wave_copy.start()
    pos_copies = []
    for n in range(chunks):
        for c in range(share):
            where = pl.ds((c * tiles + n * span) * LANES, span * LANES)
            copy = pltpu.make_async_copy(
                pos_hbm.at[:, :, where], pos.at[:, :, where], pos_sem.at[n * share + c]
            )
            copy.start()
            pos_copies.append(copy)
    label_copy = pltpu.make_async_copy(label_hbm, label_in, in_sem.at[1])
    label_copy.start()
    value_copy = pltpu.make_async_copy(values_hbm, values, in_sem.at[2])
    value_copy.start()

    lane = lax.broadcasted_iota(jnp.int32, (8, LANES), 1)
    sub = lax.broadcasted_iota(jnp.int32, (8, LANES), 0)
    first = me * local_beads
    table = cycle_table(sub.astype(jnp.float32), (first + lane).astype(jnp.float32), beads)
    columns = [jnp.broadcast_to(table[:, b : b + 1], (8, LANES)) for b in range(local_beads)]

    wave_copy.wait()
    waves[me] = jnp.zeros((8, kvec), jnp.float32)
    waves[me, 0:3, :] = wave_in[...].astype(jnp.float32)

    part_copies, wave_copies = [], []
    for n in range(chunks):
        for c in range(share):
            pos_copies[n * share + c].wait()
            for x in range(3):
                for t in range(span):
                    at = (c * tiles + n * span + t) * LANES
                    total = None
                    for b in range(local_beads):
                        term = columns[b] * pos[x, b : b + 1, at : at + LANES]
                        total = term if total is None else total + term
                    row = x * span + t
                    for j in range(CONTR):
                        part[j * share + c, n, row : row + 1, :] = total[j : j + 1, :]
        if n == 0:
            pl.semaphore_wait(barrier, len(peers))
            for d in range(1, nb):
                copy = pltpu.make_async_remote_copy(
                    src_ref=waves.at[me], dst_ref=waves.at[me], send_sem=send_wave.at[d],
                    recv_sem=recv_wave.at[d], device_id=bead_peer(d), device_id_type=MESH,
                )
                copy.start()
                wave_copies.append(copy)
        for d in range(1, nb):
            peer = bead_peer(d)
            copy = pltpu.make_async_remote_copy(
                src_ref=part.at[peer[0], n], dst_ref=land.at[d, n], send_sem=send_part.at[n, d],
                recv_sem=recv_part.at[n, d], device_id=peer, device_id_type=MESH,
            )
            copy.start()
            part_copies.append(copy)
    label_copy.wait()
    value_copy.wait()
    label = label_in[...]
    q = jnp.zeros(label.shape, jnp.float32)
    for kind in range(values.shape[0]):
        q = q + jnp.where(label == kind, values[kind], 0.0)
    for c in range(share):
        charge[c, 0:tiles, :] = q[c * tiles : (c + 1) * tiles, :]

    row_id = lax.broadcasted_iota(jnp.int32, (ROWS, LANES), 0)
    second = jnp.where(row_id < ROWS - REACH, row_id, row_id - ROWS).astype(jnp.float32)
    third = (row_id - REACH).astype(jnp.float32)

    for n in range(chunks):
        for copy in part_copies[n * (nb - 1) : (n + 1) * (nb - 1)]:
            copy.wait()
        total = part[me, n]
        for d in range(1, nb):
            total = total + land[d, n]
        site[n] = total - jnp.round(total)

        def build(t, carry, n=n):
            where = pl.ds(pl.multiple_of((n * span + t) * LANES, LANES), LANES)
            x = site[n, pl.ds(t, 1), :]
            step_r = jnp.broadcast_to(cos_turns(x), (ROWS, LANES))
            step_i = jnp.broadcast_to(sin_turns(x), (ROWS, LANES))
            y = second * site[n, pl.ds(span + t, 1), :]
            z = third * site[n, pl.ds(2 * span + t, 1), :]
            real, imag = cos_turns(y), sin_turns(y)
            reals, imags = [real[:HALF]], [imag[:HALF]]
            for a in range(REACH):
                real, imag = real * step_r - imag * step_i, real * step_i + imag * step_r
                reals.append(real)
                imags.append(imag)
            for base, parts in ((0, reals), (GRID, imags)):
                blocks = [parts[0]]
                for a in range(1, REACH + 1, 2):
                    blocks.append(jnp.concatenate(parts[a : a + 2], axis=0))
                at = base
                for block in blocks:
                    high, low = split(block)
                    xy_high[at : at + block.shape[0], where] = high
                    xy_low[at : at + block.shape[0], where] = low
                    at += block.shape[0]
            cos_z, sin_z = cos_turns(z), sin_turns(z)
            z_wave[0, :, where] = cos_z
            z_wave[1, :, where] = sin_z
            q_row = charge[chunk, pl.ds(n * span + t, 1), :]
            qc, qs = q_row * cos_z, q_row * sin_z
            for i, block in enumerate(((qc, qs), (-qs, qc))):
                high, low = split(jnp.concatenate(block, axis=0))
                z_mat[i, 0 : 2 * ROWS, where] = high
                z_mat[i, 2 * ROWS : 4 * ROWS, where] = low
            return carry

        lax.fori_loop(0, span, build, 0)

    pieces = factor_land.shape[1] // group
    count_tiles = 2 * ROWS * GRID // (8 * LANES)
    product = dot_nt(z_mat[0], xy_high[0:GRID, :]) + dot_nt(z_mat[1], xy_high[GRID : 2 * GRID, :])
    own = product[: 2 * ROWS] + product[2 * ROWS :]
    own = own + dot_nt(z_mat[0, 0 : 2 * ROWS, :], xy_low[0:GRID, :])
    own = own + dot_nt(z_mat[1, 0 : 2 * ROWS, :], xy_low[GRID : 2 * GRID, :])
    for l in range(GRID // LANES):
        for i in range(2 * ROWS // 8):
            factor[l * (2 * ROWS // 8) + i] = own[8 * i : 8 * i + 8, l * LANES : (l + 1) * LANES]
    for i in range(count_tiles, group * pieces):
        factor[i] = jnp.zeros((8, LANES), jnp.float32)
    factor_copies = []
    for d in range(1, group):
        peer = group_peer(d)
        target = peer[1] * share + lax.rem(peer[0], share)
        copy = pltpu.make_async_remote_copy(
            src_ref=factor, dst_ref=factor_land.at[d],
            send_sem=send_fac.at[d], recv_sem=recv_fac.at[d], device_id=peer, device_id_type=MESH,
        )
        copy.start()
        factor_copies.append(copy)

    for copy in wave_copies:
        copy.wait()
    count = jnp.zeros((ROWS, GRID), jnp.float32)
    pair_id = lax.broadcasted_iota(jnp.int32, (GRID, kvec), 0).astype(jnp.float32)
    third_id = lax.broadcasted_iota(jnp.int32, (ROWS, kvec), 0).astype(jnp.float32)
    for n in range(nb):
        m = waves[n]
        m0, m1, m2 = m[0:1], m[1:2], m[2:3]
        wrapped = jnp.where(m1 < 0.0, m1 + ROWS, m1)
        pair = jnp.where(m0 > 0.0, HALF + (m0 - 1.0) * ROWS + wrapped, m1)
        hot_pair = jnp.where(pair_id == pair, 1.0, 0.0).astype(jnp.bfloat16)
        hot_third = jnp.where(third_id == m2 + REACH, 1.0, 0.0).astype(jnp.bfloat16)
        count = count + dot_nt(hot_third, hot_pair)


    for copy in factor_copies:
        copy.wait()
    total = factor[...]
    for d in range(1, group):
        total = total + factor_land[d]
    whole[...] = total

    col = lax.broadcasted_iota(jnp.int32, (ROWS, GRID), 1)
    line = lax.broadcasted_iota(jnp.int32, (ROWS, GRID), 0)
    f0 = jnp.zeros((ROWS, GRID), jnp.int32)
    for a in range(REACH):
        f0 = f0 + jnp.where(col >= HALF + a * ROWS, 1, 0)
    f1 = jnp.where(f0 > 0, col - HALF - (f0 - 1) * ROWS, col)
    f1 = jnp.where(f1 < ROWS - REACH, f1, f1 - ROWS)
    f2 = line - REACH
    f0, f1, f2 = f0.astype(jnp.float32), f1.astype(jnp.float32), f2.astype(jnp.float32)
    msq = f0 * f0 + f1 * f1 + f2 * f2
    weight = 4.0 * jnp.exp(-msq / 100.0) / (jnp.maximum(msq, 1.0) * float(sites * na))
    weight = weight * count
    w0, w1 = jnp.concatenate([f0, f0], axis=1), jnp.concatenate([f1, f1], axis=1)

    per_lane = 2 * ROWS // 8
    half = per_lane // 2

    def gather(base):
        return jnp.concatenate(
            [
                jnp.concatenate([whole[l * per_lane + base + i] for i in range(half)], axis=0)
                for l in range(GRID // LANES)
            ],
            axis=1,
        )

    gr, gi = weight * gather(0), weight * gather(half)
    u, v = jnp.concatenate([-gi, gr], axis=1), jnp.concatenate([gr, gi], axis=1)
    left = jnp.concatenate([u, v, w0 * u, w0 * v, w1 * u, w1 * v], axis=0)
    left_high, left_low = split(left)
    left_both = jnp.concatenate([left_high, left_low], axis=0)
    height = 6 * ROWS

    width = 2 * LANES if span % 2 == 0 else LANES
    per = width // LANES
    m2_rows = (lax.broadcasted_iota(jnp.int32, (ROWS, width), 0) - REACH).astype(jnp.float32)
    force_copies = []
    for n in range(chunks):
        for k in range(span // per):
            start = (n * span + k * per) * LANES
            where = slice(start, start + width)
            both = dot_nn(left_both, xy_high[:, where])
            term = both[:height] + both[height:] + dot_nn(left_high, xy_low[:, where])
            cz, sz = z_wave[0, :, where], z_wave[1, :, where]
            blocks = [
                term[2 * i * ROWS : (2 * i + 1) * ROWS] * cz
                + term[(2 * i + 1) * ROWS : (2 * i + 2) * ROWS] * sz
                for i in range(3)
            ]
            along = (blocks[1], blocks[2], blocks[0] * m2_rows)
            for x in range(3):
                summed = TWO_PI * jnp.sum(along[x], axis=0, keepdims=True)
                for p in range(per):
                    t = k * per + p
                    q_row = charge[chunk, n * span + t : n * span + t + 1, :]
                    force[n, x * span + t : x * span + t + 1, :] = (
                        q_row * summed[:, p * LANES : (p + 1) * LANES]
                    )
        for d in range(1, nb):
            copy = pltpu.make_async_remote_copy(
                src_ref=force.at[n], dst_ref=gathered.at[me, n], send_sem=send_force.at[n, d],
                recv_sem=recv_force.at[n, d], device_id=bead_peer(d), device_id_type=MESH,
            )
            copy.start()
            force_copies.append(copy)

    own_copy = pltpu.make_async_copy(force, gathered.at[me], in_sem.at[3])
    own_copy.start()
    for copy in force_copies:
        copy.wait()
    own_copy.wait()


def expand(nb, force_hbm, out_hbm, force, out, in_sem, out_sem):
    share = nb // CONTR
    chunks = force.shape[1]
    local_beads, sites = out.shape[1], out.shape[2]
    tiles = sites // share // LANES
    span = tiles // chunks
    copy_in = pltpu.make_async_copy(force_hbm, force, in_sem)
    copy_in.start()
    first = lax.axis_index("bead") * local_beads
    sub = lax.broadcasted_iota(jnp.int32, (local_beads, LANES), 0)
    lane = lax.broadcasted_iota(jnp.int32, (local_beads, LANES), 1)
    table = cycle_table(
        lane.astype(jnp.float32), (first + sub).astype(jnp.float32), local_beads * nb
    )
    spread = [jnp.broadcast_to(table[:, j : j + 1], (local_beads, LANES)) for j in range(CONTR)]
    copy_in.wait()
    copies = []
    for x in range(3):
        for c in range(share):
            for t in range(tiles):
                total = None
                for j in range(CONTR):
                    row = x * span + t % span
                    term = spread[j] * force[j * share + c, t // span, row : row + 1, :]
                    total = term if total is None else total + term
                at = (c * tiles + t) * LANES
                out[x, :, at : at + LANES] = total
        copy = pltpu.make_async_copy(out.at[x], out_hbm.at[x], out_sem.at[x])
        copy.start()
        copies.append(copy)
    for copy in copies:
        copy.wait()


def local(nb, na, positions, waves, labels, values):
    local_beads, _, sites = positions.shape
    kvec = waves.shape[1]
    share = nb // CONTR
    own_sites = sites // share
    tiles = own_sites // LANES
    span = tiles
    chunks = tiles // span
    rows = -(-3 * span // 8) * 8
    group = na * share
    pieces = -(-(2 * ROWS * GRID // (8 * LANES)) // group)
    dma = pltpu.SemaphoreType.DMA
    f32, bf16 = jnp.float32, jnp.bfloat16
    hbm = pl.BlockSpec(memory_space=pltpu.HBM)
    gathered = pl.pallas_call(
        functools.partial(kernel, nb, na),
        out_shape=jax.ShapeDtypeStruct((nb, chunks, rows, LANES), f32),
        in_specs=[hbm] * 4,
        out_specs=hbm,
        scratch_shapes=[
            pltpu.SMEM(values.shape, f32),
            pltpu.VMEM((3, local_beads, sites), f32),
            pltpu.VMEM((3, kvec), jnp.int32),
            pltpu.VMEM((sites // LANES, LANES), jnp.int32),
            pltpu.VMEM((nb, chunks, rows, LANES), f32),
            pltpu.VMEM((nb, chunks, rows, LANES), f32),
            pltpu.VMEM((chunks, rows, LANES), f32),
            pltpu.VMEM((nb, 8, kvec), f32),
            pltpu.VMEM((share, -(-tiles // 8) * 8, LANES), f32),
            pltpu.VMEM((2 * GRID, own_sites), bf16),
            pltpu.VMEM((2 * GRID, own_sites), bf16),
            pltpu.VMEM((2, 4 * ROWS, own_sites), bf16),
            pltpu.VMEM((2, ROWS, own_sites), f32),
            pltpu.VMEM((group * pieces, 8, LANES), f32),
            pltpu.VMEM((group, group * pieces, 8, LANES), f32),
            pltpu.VMEM((group * pieces, 8, LANES), f32),
            pltpu.VMEM((chunks, rows, LANES), f32),
            dma((4,)), dma((chunks * share,)), dma((nb,)), dma((nb,)), dma((chunks, nb)), dma((chunks, nb)),
            dma((group,)), dma((group,)), dma((chunks, nb)), dma((chunks, nb)),
        ],
        compiler_params=pltpu.CompilerParams(
            collective_id=0, has_side_effects=True, vmem_limit_bytes=60 * 1024 * 1024
        ),
    )(values, jnp.transpose(positions, (1, 0, 2)), waves, labels.reshape(-1, LANES))
    out = pl.pallas_call(
        functools.partial(expand, nb),
        out_shape=jax.ShapeDtypeStruct((3, local_beads, sites), f32),
        in_specs=[hbm],
        out_specs=hbm,
        scratch_shapes=[
            pltpu.VMEM((nb, chunks, rows, LANES), f32),
            pltpu.VMEM((3, local_beads, sites), f32),
            dma, dma((3,)),
        ],
        compiler_params=pltpu.CompilerParams(vmem_limit_bytes=60 * 1024 * 1024),
    )(gathered)
    return jnp.transpose(out, (1, 0, 2))


def solution(mesh):
    in_specs = (P("bead", None, "atom"), P(None, "bead"), P("atom"), P())
    out_specs = P("bead", None, "atom")
    body = functools.partial(local, mesh.shape["bead"], mesh.shape["atom"])
    return jax.shard_map(body, mesh=mesh, in_specs=in_specs, out_specs=out_specs, check_vma=False)
```

```python
import functools
import math

import jax
import jax.numpy as jnp
import numpy as np
from jax import lax
from jax.experimental import pallas as pl
from jax.experimental.pallas import tpu as pltpu
from jax.sharding import PartitionSpec as P

CONTR = 8
REACH = 10
ROWS = 24
HALF = 16
GRID = HALF + REACH * ROWS
TWO_PI = 2.0 * math.pi
MESH = pl.DeviceIdType.MESH
LANES = 128


def _sine_coefficients():
    u = np.cos(np.pi * (np.arange(400) + 0.5) / 400)
    square = 0.125 + 0.125 * u
    r = np.sqrt(square)
    value = np.sin(2 * np.pi * r) / (r * (0.25 - square))
    return [float(c) for c in np.polynomial.polynomial.polyfit(square, value, 5)]


SINE = _sine_coefficients()


def sin_turns(turns):
    r = turns - jnp.round(turns)
    square = r * r
    p = SINE[5]
    for c in SINE[4::-1]:
        p = p * square + c
    return r * (0.25 - square) * p


def cos_turns(turns):
    return sin_turns(turns + 0.25)


def split(value):
    high = value.astype(jnp.bfloat16)
    low = (value - high.astype(jnp.float32)).astype(jnp.bfloat16)
    return high, low


def cycle_table(j, b, beads):
    shift = j / CONTR - b / beads
    total = jnp.ones_like(shift)
    for c in range(1, CONTR // 2):
        total = total + 2.0 * cos_turns(c * shift)
    last = cos_turns(0.5 * j) * cos_turns((CONTR // 2) * b / beads)
    total = total + math.sqrt(2.0) * last
    return total / beads


def dot_nn(a, b):
    return lax.dot_general(a, b, (((1,), (0,)), ((), ())), preferred_element_type=jnp.float32)


def dot_nt(a, b):
    return lax.dot_general(a, b, (((1,), (1,)), ((), ())), preferred_element_type=jnp.float32)


def kernel(
    nb, na, values_hbm, pos_hbm, wave_hbm, label_hbm, gathered,
    values, pos, wave_in, label_in,
    part, land, site, waves, charge, xy_high, xy_low, z_mat, z_wave, factor, factor_land, whole, force,
    in_sem, pos_sem, send_wave, recv_wave, send_part, recv_part, send_fac, recv_fac,
    send_force, recv_force,
):
    share = nb // CONTR
    local_beads, sites = pos.shape[1], pos.shape[2]
    beads = local_beads * nb
    own_sites = sites // share
    tiles = own_sites // LANES
    chunks = site.shape[0]
    span = tiles // chunks
    kvec = wave_in.shape[1]
    group = na * share
    me = lax.axis_index("bead")
    atom = lax.axis_index("atom")
    bead, chunk = me // share, lax.rem(me, share)
    place = atom * share + chunk

    def bead_peer(d):
        return (lax.rem(me + d, nb), atom)

    def group_peer(d):
        other = bead * share + lax.rem(chunk + d % share, share)
        return (other, lax.rem(atom + d // share, na))

    barrier = pltpu.get_barrier_semaphore()
    peers = [bead_peer(d) for d in range(1, nb)]
    peers += [group_peer(d) for d in range(1, group) if d >= share]
    for peer in peers:
        pl.semaphore_signal(barrier, inc=1, device_id=peer, device_id_type=MESH)

    wave_copy = pltpu.make_async_copy(wave_hbm, wave_in, in_sem.at[0])
    wave_copy.start()
    pos_copies = []
    for n in range(chunks):
        for c in range(share):
            where = pl.ds((c * tiles + n * span) * LANES, span * LANES)
            copy = pltpu.make_async_copy(
                pos_hbm.at[:, :, where], pos.at[:, :, where], pos_sem.at[n * share + c]
            )
            copy.start()
            pos_copies.append(copy)
    label_copy = pltpu.make_async_copy(label_hbm, label_in, in_sem.at[1])
    label_copy.start()
    value_copy = pltpu.make_async_copy(values_hbm, values, in_sem.at[2])
    value_copy.start()

    lane = lax.broadcasted_iota(jnp.int32, (8, LANES), 1)
    sub = lax.broadcasted_iota(jnp.int32, (8, LANES), 0)
    first = me * local_beads
    table = cycle_table(sub.astype(jnp.float32), (first + lane).astype(jnp.float32), beads)
    columns = [jnp.broadcast_to(table[:, b : b + 1], (8, LANES)) for b in range(local_beads)]

    wave_copy.wait()
    waves[me] = jnp.zeros((8, kvec), jnp.float32)
    waves[me, 0:3, :] = wave_in[...].astype(jnp.float32)

    part_copies, wave_copies = [], []
    for n in range(chunks):
        for c in range(share):
            pos_copies[n * share + c].wait()
            for x in range(3):
                for t in range(span):
                    at = (c * tiles + n * span + t) * LANES
                    total = None
                    for b in range(local_beads):
                        term = columns[b] * pos[x, b : b + 1, at : at + LANES]
                        total = term if total is None else total + term
                    row = x * span + t
                    for j in range(CONTR):
                        part[j * share + c, n, row : row + 1, :] = total[j : j + 1, :]
        if n == 0:
            pl.semaphore_wait(barrier, len(peers))
            for d in range(1, nb):
                copy = pltpu.make_async_remote_copy(
                    src_ref=waves.at[me], dst_ref=waves.at[me], send_sem=send_wave.at[d],
                    recv_sem=recv_wave.at[d], device_id=bead_peer(d), device_id_type=MESH,
                )
                copy.start()
                wave_copies.append(copy)
        for d in range(1, nb):
            peer = bead_peer(d)
            copy = pltpu.make_async_remote_copy(
                src_ref=part.at[peer[0], n], dst_ref=land.at[d, n], send_sem=send_part.at[n, d],
                recv_sem=recv_part.at[n, d], device_id=peer, device_id_type=MESH,
            )
            copy.start()
            part_copies.append(copy)
    label_copy.wait()
    value_copy.wait()
    label = label_in[...]
    q = jnp.zeros(label.shape, jnp.float32)
    for kind in range(values.shape[0]):
        q = q + jnp.where(label == kind, values[kind], 0.0)
    for c in range(share):
        charge[c, 0:tiles, :] = q[c * tiles : (c + 1) * tiles, :]

    row_id = lax.broadcasted_iota(jnp.int32, (ROWS, LANES), 0)
    second = jnp.where(row_id < ROWS - REACH, row_id, row_id - ROWS).astype(jnp.float32)
    third = (row_id - REACH).astype(jnp.float32)

    for n in range(chunks):
        for copy in part_copies[n * (nb - 1) : (n + 1) * (nb - 1)]:
            copy.wait()
        total = part[me, n]
        for d in range(1, nb):
            total = total + land[d, n]
        site[n] = total - jnp.round(total)

        def build(t, carry, n=n):
            where = pl.ds(pl.multiple_of((n * span + t) * LANES, LANES), LANES)
            x = site[n, pl.ds(t, 1), :]
            step_r = jnp.broadcast_to(cos_turns(x), (ROWS, LANES))
            step_i = jnp.broadcast_to(sin_turns(x), (ROWS, LANES))
            y = second * site[n, pl.ds(span + t, 1), :]
            z = third * site[n, pl.ds(2 * span + t, 1), :]
            real, imag = cos_turns(y), sin_turns(y)
            reals, imags = [real[:HALF]], [imag[:HALF]]
            for a in range(REACH):
                real, imag = real * step_r - imag * step_i, real * step_i + imag * step_r
                reals.append(real)
                imags.append(imag)
            for base, parts in ((0, reals), (GRID, imags)):
                blocks = [parts[0]]
                for a in range(1, REACH + 1, 2):
                    blocks.append(jnp.concatenate(parts[a : a + 2], axis=0))
                at = base
                for block in blocks:
                    high, low = split(block)
                    xy_high[at : at + block.shape[0], where] = high
                    xy_low[at : at + block.shape[0], where] = low
                    at += block.shape[0]
            cos_z, sin_z = cos_turns(z), sin_turns(z)
            z_wave[0, :, where] = cos_z
            z_wave[1, :, where] = sin_z
            q_row = charge[chunk, pl.ds(n * span + t, 1), :]
            qc, qs = q_row * cos_z, q_row * sin_z
            for i, block in enumerate(((qc, qs), (-qs, qc))):
                high, low = split(jnp.concatenate(block, axis=0))
                z_mat[i, 0 : 2 * ROWS, where] = high
                z_mat[i, 2 * ROWS : 4 * ROWS, where] = low
            return carry

        lax.fori_loop(0, span, build, 0)

    pieces = factor_land.shape[1] // group
    count_tiles = 2 * ROWS * GRID // (8 * LANES)
    product = dot_nt(z_mat[0], xy_high[0:GRID, :]) + dot_nt(z_mat[1], xy_high[GRID : 2 * GRID, :])
    own = product[: 2 * ROWS] + product[2 * ROWS :]
    own = own + dot_nt(z_mat[0, 0 : 2 * ROWS, :], xy_low[0:GRID, :])
    own = own + dot_nt(z_mat[1, 0 : 2 * ROWS, :], xy_low[GRID : 2 * GRID, :])
    for l in range(GRID // LANES):
        for i in range(2 * ROWS // 8):
            factor[l * (2 * ROWS // 8) + i] = own[8 * i : 8 * i + 8, l * LANES : (l + 1) * LANES]
    for i in range(count_tiles, group * pieces):
        factor[i] = jnp.zeros((8, LANES), jnp.float32)
    factor_copies = []
    for d in range(1, group):
        peer = group_peer(d)
        target = peer[1] * share + lax.rem(peer[0], share)
        copy = pltpu.make_async_remote_copy(
            src_ref=factor, dst_ref=factor_land.at[d],
            send_sem=send_fac.at[d], recv_sem=recv_fac.at[d], device_id=peer, device_id_type=MESH,
        )
        copy.start()
        factor_copies.append(copy)

    for copy in wave_copies:
        copy.wait()
    count = jnp.zeros((ROWS, GRID), jnp.float32)
    pair_id = lax.broadcasted_iota(jnp.int32, (GRID, kvec), 0).astype(jnp.float32)
    third_id = lax.broadcasted_iota(jnp.int32, (ROWS, kvec), 0).astype(jnp.float32)
    for n in range(nb):
        m = waves[n]
        m0, m1, m2 = m[0:1], m[1:2], m[2:3]
        wrapped = jnp.where(m1 < 0.0, m1 + ROWS, m1)
        pair = jnp.where(m0 > 0.0, HALF + (m0 - 1.0) * ROWS + wrapped, m1)
        hot_pair = jnp.where(pair_id == pair, 1.0, 0.0).astype(jnp.bfloat16)
        hot_third = jnp.where(third_id == m2 + REACH, 1.0, 0.0).astype(jnp.bfloat16)
        count = count + dot_nt(hot_third, hot_pair)

    col = lax.broadcasted_iota(jnp.int32, (ROWS, GRID), 1)
    line = lax.broadcasted_iota(jnp.int32, (ROWS, GRID), 0)
    f0 = jnp.zeros((ROWS, GRID), jnp.int32)
    for a in range(REACH):
        f0 = f0 + jnp.where(col >= HALF + a * ROWS, 1, 0)
    f1 = jnp.where(f0 > 0, col - HALF - (f0 - 1) * ROWS, col)
    f1 = jnp.where(f1 < ROWS - REACH, f1, f1 - ROWS)
    f2 = line - REACH
    f0, f1, f2 = f0.astype(jnp.float32), f1.astype(jnp.float32), f2.astype(jnp.float32)
    msq = f0 * f0 + f1 * f1 + f2 * f2
    weight = 4.0 * jnp.exp(-msq / 100.0) / (jnp.maximum(msq, 1.0) * float(sites * na))
    weight = weight * count
    w0, w1 = jnp.concatenate([f0, f0], axis=1), jnp.concatenate([f1, f1], axis=1)

    for copy in factor_copies:
        copy.wait()
    total = factor[...]
    for d in range(1, group):
        total = total + factor_land[d]
    whole[...] = total

    per_lane = 2 * ROWS // 8
    half = per_lane // 2

    def gather(base):
        return jnp.concatenate(
            [
                jnp.concatenate([whole[l * per_lane + base + i] for i in range(half)], axis=0)
                for l in range(GRID // LANES)
            ],
            axis=1,
        )

    gr, gi = weight * gather(0), weight * gather(half)
    u, v = jnp.concatenate([-gi, gr], axis=1), jnp.concatenate([gr, gi], axis=1)
    left = jnp.concatenate([u, v, w0 * u, w0 * v, w1 * u, w1 * v], axis=0)
    left_high, left_low = split(left)
    left_both = jnp.concatenate([left_high, left_low], axis=0)
    height = 6 * ROWS

    width = 2 * LANES if span % 2 == 0 else LANES
    per = width // LANES
    m2_rows = (lax.broadcasted_iota(jnp.int32, (ROWS, width), 0) - REACH).astype(jnp.float32)
    force_copies = []
    for n in range(chunks):
        for k in range(span // per):
            start = (n * span + k * per) * LANES
            where = slice(start, start + width)
            both = dot_nn(left_both, xy_high[:, where])
            term = both[:height] + both[height:] + dot_nn(left_high, xy_low[:, where])
            cz, sz = z_wave[0, :, where], z_wave[1, :, where]
            blocks = [
                term[2 * i * ROWS : (2 * i + 1) * ROWS] * cz
                + term[(2 * i + 1) * ROWS : (2 * i + 2) * ROWS] * sz
                for i in range(3)
            ]
            along = (blocks[1], blocks[2], blocks[0] * m2_rows)
            for x in range(3):
                summed = TWO_PI * jnp.sum(along[x], axis=0, keepdims=True)
                for p in range(per):
                    t = k * per + p
                    q_row = charge[chunk, n * span + t : n * span + t + 1, :]
                    force[n, x * span + t : x * span + t + 1, :] = (
                        q_row * summed[:, p * LANES : (p + 1) * LANES]
                    )
        for d in range(1, nb):
            copy = pltpu.make_async_remote_copy(
                src_ref=force.at[n], dst_ref=gathered.at[me, n], send_sem=send_force.at[n, d],
                recv_sem=recv_force.at[n, d], device_id=bead_peer(d), device_id_type=MESH,
            )
            copy.start()
            force_copies.append(copy)

    own_copy = pltpu.make_async_copy(force, gathered.at[me], in_sem.at[3])
    own_copy.start()
    for copy in force_copies:
        copy.wait()
    own_copy.wait()


def expand(nb, force_hbm, out_hbm, force, out, in_sem, out_sem):
    share = nb // CONTR
    chunks = force.shape[1]
    local_beads, sites = out.shape[1], out.shape[2]
    tiles = sites // share // LANES
    span = tiles // chunks
    copy_in = pltpu.make_async_copy(force_hbm, force, in_sem)
    copy_in.start()
    first = lax.axis_index("bead") * local_beads
    sub = lax.broadcasted_iota(jnp.int32, (local_beads, LANES), 0)
    lane = lax.broadcasted_iota(jnp.int32, (local_beads, LANES), 1)
    table = cycle_table(
        lane.astype(jnp.float32), (first + sub).astype(jnp.float32), local_beads * nb
    )
    spread = [jnp.broadcast_to(table[:, j : j + 1], (local_beads, LANES)) for j in range(CONTR)]
    copy_in.wait()
    copies = []
    for x in range(3):
        for c in range(share):
            for t in range(tiles):
                total = None
                for j in range(CONTR):
                    row = x * span + t % span
                    term = spread[j] * force[j * share + c, t // span, row : row + 1, :]
                    total = term if total is None else total + term
                at = (c * tiles + t) * LANES
                out[x, :, at : at + LANES] = total
        copy = pltpu.make_async_copy(out.at[x], out_hbm.at[x], out_sem.at[x])
        copy.start()
        copies.append(copy)
    for copy in copies:
        copy.wait()


def local(nb, na, positions, waves, labels, values):
    local_beads, _, sites = positions.shape
    kvec = waves.shape[1]
    share = nb // CONTR
    own_sites = sites // share
    tiles = own_sites // LANES
    span = tiles
    chunks = tiles // span
    rows = -(-3 * span // 8) * 8
    group = na * share
    pieces = -(-(2 * ROWS * GRID // (8 * LANES)) // group)
    dma = pltpu.SemaphoreType.DMA
    f32, bf16 = jnp.float32, jnp.bfloat16
    hbm = pl.BlockSpec(memory_space=pltpu.HBM)
    gathered = pl.pallas_call(
        functools.partial(kernel, nb, na),
        out_shape=jax.ShapeDtypeStruct((nb, chunks, rows, LANES), f32),
        in_specs=[hbm] * 4,
        out_specs=hbm,
        scratch_shapes=[
            pltpu.SMEM(values.shape, f32),
            pltpu.VMEM((3, local_beads, sites), f32),
            pltpu.VMEM((3, kvec), jnp.int32),
            pltpu.VMEM((sites // LANES, LANES), jnp.int32),
            pltpu.VMEM((nb, chunks, rows, LANES), f32),
            pltpu.VMEM((nb, chunks, rows, LANES), f32),
            pltpu.VMEM((chunks, rows, LANES), f32),
            pltpu.VMEM((nb, 8, kvec), f32),
            pltpu.VMEM((share, -(-tiles // 8) * 8, LANES), f32),
            pltpu.VMEM((2 * GRID, own_sites), bf16),
            pltpu.VMEM((2 * GRID, own_sites), bf16),
            pltpu.VMEM((2, 4 * ROWS, own_sites), bf16),
            pltpu.VMEM((2, ROWS, own_sites), f32),
            pltpu.VMEM((group * pieces, 8, LANES), f32),
            pltpu.VMEM((group, group * pieces, 8, LANES), f32),
            pltpu.VMEM((group * pieces, 8, LANES), f32),
            pltpu.VMEM((chunks, rows, LANES), f32),
            dma((4,)), dma((chunks * share,)), dma((nb,)), dma((nb,)), dma((chunks, nb)), dma((chunks, nb)),
            dma((group,)), dma((group,)), dma((chunks, nb)), dma((chunks, nb)),
        ],
        compiler_params=pltpu.CompilerParams(
            collective_id=0, has_side_effects=True, vmem_limit_bytes=60 * 1024 * 1024
        ),
    )(values, jnp.transpose(positions, (1, 0, 2)), waves, labels.reshape(-1, LANES))
    out = pl.pallas_call(
        functools.partial(expand, nb),
        out_shape=jax.ShapeDtypeStruct((3, local_beads, sites), f32),
        in_specs=[hbm],
        out_specs=hbm,
        scratch_shapes=[
            pltpu.VMEM((nb, chunks, rows, LANES), f32),
            pltpu.VMEM((3, local_beads, sites), f32),
            dma, dma((3,)),
        ],
        compiler_params=pltpu.CompilerParams(vmem_limit_bytes=60 * 1024 * 1024),
    )(gathered)
    return jnp.transpose(out, (1, 0, 2))


def solution(mesh):
    in_specs = (P("bead", None, "atom"), P(None, "bead"), P("atom"), P())
    out_specs = P("bead", None, "atom")
    body = functools.partial(local, mesh.shape["bead"], mesh.shape["atom"])
    return jax.shard_map(body, mesh=mesh, in_specs=in_specs, out_specs=out_specs, check_vma=False)
```
